512 devices in a mesh: ka: 64 (over z_lo, x, core), vert: 8 (over y, z_hi).
Axes of the slice: x: 4, y: 4, z: 16 (z_hi: 2, z_lo: 8; z = z_hi * 8 + z_lo), core: 2. Of those that a mesh axis runs over, the one named last changes fastest.
Arguments:
- amplitudes: bfloat16 [2, 64, 4, 2, 128, 128], P(None, 'ka', None, None, 'vert'), may hold values from -6 to 6
- factors: bfloat16 [2, 64, 2, 24, 128, 128], P(None, 'ka', None, 'vert'), may hold values from -0.109375 to 0.109375
- kminus: int32 [64, 64], replicated, may hold values from 0 to 63, as said below
- kj_rows: int32 [2], replicated, may hold values from 0 to 63
- kshift: int32 [1], replicated, may hold values from 0 to 63
Outputs:
- sigma: bfloat16 [2, 64, 4, 2, 128, 128], P(None, 'ka', None, None, 'vert')
The draws below stay inside these ranges and needn't reach their ends.
Inputs may be any that keep to these rules, and one draw needn't show every extreme that they name: kminus[x, y] is the label of the difference x - y in the group of the 64 k-points of a mesh of side 4 in each direction, under a labelling drawn once; each row and column is a permutation.
All inputs are finite; a program needn't handle non-finite values.
Results may differ from the reference program's by a relative error of at most 0.0058.
Values may be sent and summed in bfloat16 or wider, within the bound.
No kernel may reach another device: no remote copies, remote signals or barrier semaphores. Data moves between devices by JAX's collectives and lax.ppermute only.
A program may use at most 64 MiB of HBM per device.

```python
import jax
import jax.numpy as jnp
from jax import lax

V = 128
OCC = 4
AUX_DEV = 3
STEPS = 2
NROW = 2
NK = 64
AUX = 24


def draw_kminus(key, part):
    key = jax.random.fold_in(key, 7)
    digits = (NK.bit_length() - 1) // 2
    labels = jax.random.permutation(key, NK).astype(jnp.int32)
    element = jnp.argsort(labels, stable=True).astype(jnp.int32)
    first = element[:, None]
    second = element[None, :]
    difference = jnp.zeros((NK, NK), jnp.int32)
    for place in range(digits):
        base = 4 ** place
        digit = jnp.mod(first // base - second // base, 4)
        difference = difference + digit * base
    return labels[difference].astype(jnp.int32)


def steps_of(key, extent, pieces, smallest, top_value):
    def one(position, blocks):
        heights = jax.random.uniform(jax.random.fold_in(jax.random.fold_in(key, 6), position), (blocks,), jnp.float32, smallest / len(pieces), top_value / len(pieces))
        return jnp.repeat(jnp.exp(heights), extent[position] // blocks).reshape((-1,) + (1,) * (len(extent) - position - 1))

    level = one(*pieces[0])
    for cut in pieces[1:]:
        level = level * one(*cut)
    return level


def normal_values(key, dims, spread, limit, shards=(), held_as=jnp.bfloat16):
    result = jax.random.normal(key, dims, jnp.float32) * spread
    if len(shards) > 0:
        result = steps_of(key, dims, shards, -0.22, 0.18) * result
    return jnp.clip(result, min=-limit, max=limit).astype(held_as)


def setup_inputs(seed: int = 0) -> dict:
    streams_of = jax.random.split(jax.random.key(seed), 6)
    amplitudes = normal_values(streams_of[0], (NROW, NK, OCC, 2, V, V), 1.0, 6.0, ((1, 64), (4, 8)))
    factors = normal_values(streams_of[1], (STEPS, NK, 2, AUX, V, V), (8 * V * AUX_DEV) ** -0.5, 0.109375, ((1, 64), (3, 8)))
    kminus = draw_kminus(jax.random.fold_in(streams_of[5], 71), 0)
    kj_rows = jax.random.randint(streams_of[3], (NROW,), 0, NK).astype(jnp.int32)
    kshift = jax.random.randint(streams_of[4], (1,), 0, NK).astype(jnp.int32)
    return dict(amplitudes=amplitudes, factors=factors, kminus=kminus, kj_rows=kj_rows, kshift=kshift)


def ladder_block(tilde, own_factor, other_factor):
    tfl = tilde.astype(jnp.float32)
    own = own_factor.astype(jnp.float32)
    oth = other_factor.astype(jnp.float32)
    z_real = jnp.einsum('jcd,lbd->jlcb', tfl[:, 0], oth[0]) - jnp.einsum('jcd,lbd->jlcb', tfl[:, 1], oth[1])
    z_imag = jnp.einsum('jcd,lbd->jlcb', tfl[:, 0], oth[1]) + jnp.einsum('jcd,lbd->jlcb', tfl[:, 1], oth[0])
    z_real = lax.optimization_barrier(z_real.astype(jnp.bfloat16)).astype(jnp.float32)
    z_imag = lax.optimization_barrier(z_imag.astype(jnp.bfloat16)).astype(jnp.float32)
    s_real = jnp.einsum('lac,jlcb->jab', own[0], z_real) - jnp.einsum('lac,jlcb->jab', own[1], z_imag)
    s_imag = jnp.einsum('lac,jlcb->jab', own[0], z_imag) + jnp.einsum('lac,jlcb->jab', own[1], z_real)
    return jnp.stack([s_real, s_imag], axis=1)


def reference(amplitudes, factors, kminus, kj_rows, kshift):
    count = amplitudes.shape[1]
    results = []
    for row in range(NROW):
        target = kminus[kj_rows[row], kshift[0]]
        partners = kminus[target].astype(jnp.int32)
        blocks = amplitudes[row]
        mirror = blocks[partners]
        tilde = (2.0 * blocks.astype(jnp.float32) - jnp.swapaxes(mirror, 3, 4).astype(jnp.float32)).astype(jnp.bfloat16)

        def per_point(point):
            total = jnp.zeros(blocks.shape[1:], jnp.float32)
            for step in range(STEPS):
                source = jnp.mod(point - step, count).astype(jnp.int32)
                total = total + ladder_block(tilde[source], factors[step, point], factors[step, partners[point]])
            return total

        sums = lax.map(per_point, jnp.arange(count, dtype=jnp.int32))
        results.append(sums.astype(jnp.bfloat16))
    return jnp.stack(results)
```

```python
import functools

import jax
import jax.numpy as jnp
from jax import lax
from jax.experimental import pallas as pl
from jax.experimental.pallas import tpu as pltpu
from jax.sharding import PartitionSpec as P


def exchange(value, axis):
    return lax.all_to_all(value, axis, split_axis=0, concat_axis=0, tiled=True)


def pick(spread, index):
    return spread.at[index].get(mode="promise_in_bounds")


def tilde_kernel(place_ref, *refs):
    own = refs[0:4]
    mirror = refs[4:8]
    out_ref, own_all, mirror_all = refs[8:11]
    for turn in range(4):
        for half in range(2):
            start = pl.multiple_of(place_ref[turn * 2 + half], 16)
            own_all[:, pl.ds(start, 16), :] = own[turn][half]
            mirror_all[:, pl.ds(start, 16), :] = mirror[turn][half]
    for step in range(2):
        for row in range(2):
            for occ in range(4):
                for part in range(2):
                    block = ((step * 2 + row) * 4 + occ) * 2 + part
                    flipped = jnp.transpose(mirror_all[block].astype(jnp.float32))
                    value = 2.0 * own_all[block].astype(jnp.float32) - flipped
                    out_ref[
                        row, step, occ * 128 : (occ + 1) * 128, part * 128 : (part + 1) * 128
                    ] = value.astype(jnp.bfloat16)


def spin_adapted(place, own, mirror):
    return pl.pallas_call(
        tilde_kernel,
        out_shape=jax.ShapeDtypeStruct((2, 2, 512, 256), jnp.bfloat16),
        in_specs=[pl.BlockSpec(memory_space=pltpu.SMEM)]
        + [pl.BlockSpec(memory_space=pltpu.VMEM)] * 8,
        out_specs=pl.BlockSpec(memory_space=pltpu.VMEM),
        scratch_shapes=[
            pltpu.VMEM((32, 128, 128), jnp.bfloat16),
            pltpu.VMEM((32, 128, 128), jnp.bfloat16),
        ],
        compiler_params=pltpu.CompilerParams(vmem_limit_bytes=32 * 1024 * 1024),
        cost_estimate=pl.CostEstimate(flops=2000000, bytes_accessed=3200000, transcendentals=0),
        name="spin_adapted",
    )(place, *own, *mirror)


def complex_matrix(real, imag):
    return jnp.concatenate(
        [jnp.concatenate([real, -imag], 1), jnp.concatenate([imag, real], 1)], 0
    )


def ladder_kernel(tilde_ref, own_ref, other_ref, out_ref, left, right, inner):
    for step in range(2):
        for lane in range(3):
            at = (step * 3 + lane) * 256
            left[:, at : at + 256] = complex_matrix(own_ref[step, 0, lane], own_ref[step, 1, lane])
    for row in range(2):
        for step in range(2):
            for lane in range(3):
                right[lane * 256 : (lane + 1) * 256, :] = complex_matrix(
                    other_ref[row, step, 0, lane], other_ref[row, step, 1, lane]
                )
            product = lax.dot_general(
                tilde_ref[row, step],
                right[...],
                (((1,), (1,)), ((), ())),
                preferred_element_type=jnp.float32,
            ).astype(jnp.bfloat16)
            for lane in range(3):
                for part in range(2):
                    at = (step * 3 + lane) * 256 + part * 128
                    column = lane * 256 + part * 128
                    for occ in range(4):
                        inner[at : at + 128, occ * 128 : (occ + 1) * 128] = product[
                            occ * 128 : (occ + 1) * 128, column : column + 128
                        ]
        total = jnp.dot(left[...], inner[...], preferred_element_type=jnp.float32)
        total = total.astype(jnp.bfloat16)
        for part in range(2):
            for place in range(4):
                at = part * 128 + place * 32
                out_ref[place, row, part] = total[at : at + 32]


def ladder(tilde, own, other):
    return pl.pallas_call(
        ladder_kernel,
        out_shape=jax.ShapeDtypeStruct((4, 2, 2, 32, 512), jnp.bfloat16),
        in_specs=[pl.BlockSpec(memory_space=pltpu.VMEM)] * 3,
        out_specs=pl.BlockSpec(memory_space=pltpu.VMEM),
        scratch_shapes=[
            pltpu.VMEM((256, 1536), jnp.bfloat16),
            pltpu.VMEM((768, 256), jnp.bfloat16),
            pltpu.VMEM((1536, 512), jnp.bfloat16),
        ],
        compiler_params=pltpu.CompilerParams(vmem_limit_bytes=32 * 1024 * 1024),
        cost_estimate=pl.CostEstimate(
            flops=1610612736, bytes_accessed=2900000, transcendentals=0
        ),
        name="ladder",
    )(tilde, own, other)


def gathered(shard):
    other = lax.ppermute(shard, "vert", [(v, v ^ 1) for v in range(8)])
    pair = jnp.stack([shard, other])
    turns = [pair]
    for turn in range(1, 4):
        turns.append(lax.ppermute(pair, "vert", [(v, (v + 2 * turn) % 8) for v in range(8)]))
    return turns


def per_device(amplitudes, factors, kminus, kj_rows, kshift):
    spot = lax.axis_index("ka")
    vert = lax.axis_index("vert")
    partners = [kminus[kminus[kj_rows[row], kshift[0]]] for row in range(2)]
    mine = jnp.where(spot < 32, partners[0], partners[1])

    shard = amplitudes[:, 0]
    behind = lax.ppermute(shard, "ka", [(i, (i + 1) % 64) for i in range(64)])
    own = gathered(jnp.stack([shard, behind]).reshape(32, 16, 128))

    spread = exchange(shard.reshape(64, 4, 128), "ka")
    chosen = jnp.concatenate([pick(spread, mine), pick(spread, jnp.roll(mine, 1))], 1)
    both = exchange(
        jnp.concatenate([chosen, factors[:, 0].reshape(64, 24, 128)], 1), "ka"
    )
    mirror = jnp.stack([both[:, 0:4], both[:, 4:8]]).reshape(32, 16, 128)
    mirror = gathered(mirror)
    spread = both[:, 8:32]
    chosen = jnp.concatenate([pick(spread, partners[0]), pick(spread, partners[1])], 1)
    other = exchange(chosen, "ka")
    other = jnp.stack([other[:, 0:24], other[:, 24:48]]).reshape(2, 2, 2, 3, 128, 128)

    high = lax.rem(vert, 2)
    level = lax.div(vert, 2)
    place = jnp.stack(
        [
            lax.rem(level + 4 - turn, 4) * 32 + (high if half == 0 else 1 - high) * 16
            for turn in range(4)
            for half in range(2)
        ]
    ).astype(jnp.int32)
    tilde = spin_adapted(place, own, mirror)
    partial = ladder(tilde, factors[:, 0], other)

    groups = [[0, 2, 4, 6], [1, 3, 5, 7]]
    pieces = lax.all_to_all(
        partial, "vert", split_axis=0, concat_axis=0, tiled=True, axis_index_groups=groups
    )
    total = jnp.sum(pieces.astype(jnp.float32), 0).reshape(2, 2, 2, 16, 4, 128)
    keep = jnp.where(high == 0, total[:, :, 0], total[:, :, 1])
    give = jnp.where(high == 0, total[:, :, 1], total[:, :, 0]).astype(jnp.bfloat16)
    taken = lax.ppermute(give, "vert", [(v, v ^ 1) for v in range(8)])
    total = (keep + taken.astype(jnp.float32)).astype(jnp.bfloat16)
    return jnp.transpose(total, (0, 3, 1, 2, 4))[:, None]


def solution(mesh):
    in_specs = (
        P(None, "ka", None, None, "vert", None),
        P(None, "ka", None, "vert", None, None),
        P(),
        P(),
        P(),
    )
    out_specs = P(None, "ka", None, None, "vert", None)
    return jax.shard_map(
        per_device, mesh=mesh, in_specs=in_specs, out_specs=out_specs, check_vma=False
    )
```

```python
import jax
import jax.numpy as jnp
from jax import lax
from jax.experimental import pallas as pl
from jax.experimental.pallas import tpu as pltpu
from jax.sharding import PartitionSpec as P

SMEM = pl.BlockSpec(memory_space=pltpu.SMEM)
VMEM = pl.BlockSpec(memory_space=pltpu.VMEM)
HBM = pl.BlockSpec(memory_space=pltpu.HBM)


def exchange(value, axis):
    return lax.all_to_all(value, axis, split_axis=0, concat_axis=0, tiled=True)


def params(mebibytes):
    return pltpu.CompilerParams(vmem_limit_bytes=mebibytes * 1024 * 1024)


def wide(value):
    return value.astype(jnp.float32)


def tables(kminus_ref, rows_ref, shift_ref, row):
    return kminus_ref[rows_ref[row], shift_ref[0]]


def mirror_kernel(kminus_ref, rows_ref, shift_ref, row_ref, spread_ref, out_ref):
    target = tables(kminus_ref, rows_ref, shift_ref, row_ref[0])
    before = wide(spread_ref[kminus_ref[target, 63]])[24:28]
    for k in range(64):
        piece = wide(spread_ref[kminus_ref[target, k]])[24:28]
        value = jnp.concatenate([piece, before], 0).astype(jnp.bfloat16)
        out_ref[k] = value
        out_ref[64 + k] = value
        before = piece


def mirror_pieces(lookup, row, spread):
    return pl.pallas_call(
        mirror_kernel,
        out_shape=jax.ShapeDtypeStruct((128, 8, 128), jnp.bfloat16),
        in_specs=[SMEM] * 4 + [VMEM],
        out_specs=VMEM,
        compiler_params=params(16),
        cost_estimate=pl.CostEstimate(flops=0, bytes_accessed=1000000, transcendentals=0),
        name="mirror_pieces",
    )(*lookup, row, spread)


def factor_kernel(kminus_ref, rows_ref, shift_ref, spread_ref, out_ref):
    first = tables(kminus_ref, rows_ref, shift_ref, 0)
    second = tables(kminus_ref, rows_ref, shift_ref, 1)
    for k in range(64):
        block = jnp.concatenate(
            [
                wide(spread_ref[kminus_ref[first, k]])[0:24],
                wide(spread_ref[kminus_ref[second, k]])[0:24],
            ],
            0,
        )
        out_ref[k] = block.astype(jnp.bfloat16)


def factor_pieces(lookup, spread):
    return pl.pallas_call(
        factor_kernel,
        out_shape=jax.ShapeDtypeStruct((64, 48, 128), jnp.bfloat16),
        in_specs=[SMEM] * 3 + [VMEM],
        out_specs=VMEM,
        compiler_params=params(16),
        cost_estimate=pl.CostEstimate(flops=0, bytes_accessed=1300000, transcendentals=0),
        name="factor_pieces",
    )(*lookup, spread)


def tilde_kernel(place_ref, own_ref, *refs):
    turns = refs[0:4]
    out_ref, left_ref, blocks, arrived = refs[4:8]
    copies = []
    for turn in range(4):
        for high in range(2):
            start = pl.multiple_of(place_ref[turn] + high * 16, 16)
            copies.append(
                pltpu.make_async_copy(
                    turns[turn].at[:, high],
                    blocks.at[:, :, pl.ds(start, 16), :],
                    arrived.at[turn * 2 + high],
                )
            )
    for copy in copies:
        copy.start()
    for step in range(2):
        for lane in range(3):
            at = (step * 3 + lane) * 256
            left_ref[:, at : at + 256] = complex_matrix(
                own_ref[step, 0, lane], own_ref[step, 1, lane]
            )
    for copy in copies:
        copy.wait()
    for step in range(2):
        for row in range(2):
            for occ in range(4):
                for part in range(2):
                    block = (row * 4 + occ) * 2 + part
                    flipped = jnp.transpose(wide(blocks[2 + step, block]))
                    value = 2.0 * wide(blocks[step, block]) - flipped
                    out_ref[
                        row, step, occ * 128 : (occ + 1) * 128, part * 128 : (part + 1) * 128
                    ] = value.astype(jnp.bfloat16)


def spin_adapted(place, own, turns):
    return pl.pallas_call(
        tilde_kernel,
        out_shape=[
            jax.ShapeDtypeStruct((2, 2, 512, 256), jnp.bfloat16),
            jax.ShapeDtypeStruct((256, 1536), jnp.bfloat16),
        ],
        in_specs=[SMEM, VMEM] + [HBM] * 4,
        out_specs=[VMEM, VMEM],
        scratch_shapes=[
            pltpu.VMEM((4, 16, 128, 128), jnp.bfloat16),
            pltpu.SemaphoreType.DMA((8,)),
        ],
        compiler_params=params(12),
        cost_estimate=pl.CostEstimate(flops=2000000, bytes_accessed=3200000, transcendentals=0),
        name="spin_adapted",
    )(place, own, *turns)


def complex_matrix(real, imag):
    return jnp.concatenate(
        [jnp.concatenate([real, -imag], 1), jnp.concatenate([imag, real], 1)], 0
    )


def ladder_kernel(tilde_ref, left_ref, other_ref, out_ref, tilde, left, other, right, inner, here):
    copies = [
        pltpu.make_async_copy(other_ref, other, here.at[0]),
        pltpu.make_async_copy(tilde_ref, tilde, here.at[1]),
        pltpu.make_async_copy(left_ref, left, here.at[2]),
    ]
    for copy in copies:
        copy.start()
    for copy in copies:
        copy.wait()
    for row in range(2):
        factor = jnp.concatenate(
            [wide(other[m])[row * 24 : (row + 1) * 24] for m in range(64)], 0
        ).astype(jnp.bfloat16)
        for step in range(2):
            for lane in range(3):
                real = (step * 6 + lane) * 128
                imag = real + 384
                right[lane * 256 : (lane + 1) * 256, :] = complex_matrix(
                    factor[real : real + 128], factor[imag : imag + 128]
                )
            product = lax.dot_general(
                tilde[row, step],
                right[...],
                (((1,), (1,)), ((), ())),
                preferred_element_type=jnp.float32,
            ).astype(jnp.bfloat16)
            for lane in range(3):
                for part in range(2):
                    at = (step * 3 + lane) * 256 + part * 128
                    column = lane * 256 + part * 128
                    for occ in range(4):
                        inner[at : at + 128, occ * 128 : (occ + 1) * 128] = product[
                            occ * 128 : (occ + 1) * 128, column : column + 128
                        ]
        total = jnp.dot(left[...], inner[...], preferred_element_type=jnp.float32)
        total = total.astype(jnp.bfloat16)
        for occ in range(4):
            for part in range(2):
                for place in range(4):
                    at = part * 128 + place * 32
                    out_ref[place, row, occ, part] = total[
                        at : at + 32, occ * 128 : (occ + 1) * 128
                    ]


def ladder(tilde, left, other):
    return pl.pallas_call(
        ladder_kernel,
        out_shape=jax.ShapeDtypeStruct((4, 2, 4, 2, 32, 128), jnp.bfloat16),
        in_specs=[HBM] * 3,
        out_specs=VMEM,
        scratch_shapes=[
            pltpu.VMEM((2, 2, 512, 256), jnp.bfloat16),
            pltpu.VMEM((256, 1536), jnp.bfloat16),
            pltpu.VMEM((64, 48, 128), jnp.bfloat16),
            pltpu.VMEM((768, 256), jnp.bfloat16),
            pltpu.VMEM((1536, 512), jnp.bfloat16),
            pltpu.SemaphoreType.DMA((3,)),
        ],
        compiler_params=params(12),
        cost_estimate=pl.CostEstimate(
            flops=1610612736, bytes_accessed=2900000, transcendentals=0
        ),
        name="ladder",
    )(tilde, left, other)


def turned(value):
    return [value] + [
        lax.ppermute(value, "vert", [(v, (v + 2 * turn) % 8) for v in range(8)])
        for turn in range(1, 4)
    ]


def swapped(value):
    return lax.ppermute(value, "vert", [(v, v ^ 1) for v in range(8)])


def ahead(value):
    return lax.ppermute(value, "ka", [(k, (k + 1) % 64) for k in range(64)])


def per_device(amplitudes, factors, kminus, kj_rows, kshift):
    spot = lax.axis_index("ka")
    vert = lax.axis_index("vert")
    high = lax.rem(vert, 2)
    level = lax.div(vert, 2)
    lookup = (kminus, kj_rows, kshift)
    row = lax.div(spot, 32).astype(jnp.int32).reshape(1)
    place = jnp.stack([lax.rem(level + 4 - turn, 4) * 32 for turn in range(4)]).astype(jnp.int32)

    shard = amplitudes[:, 0]
    spread = exchange(
        jnp.concatenate([factors[:, 0].reshape(64, 24, 128), shard.reshape(64, 4, 128)], 1), "ka"
    )
    behind = ahead(shard)
    other_half = swapped(shard)
    spread, behind, other_half = lax.optimization_barrier((spread, behind, other_half))
    here = jnp.stack([shard, behind]).reshape(2, 16, 16, 128)
    there = jnp.stack([other_half, ahead(other_half)]).reshape(2, 16, 16, 128)
    own = jnp.where(
        high == 0, jnp.stack([here, there], axis=1), jnp.stack([there, here], axis=1)
    )
    pairs = [[k * 8 + 2 * y + h for h in range(2) for k in range(64)] for y in range(4)]
    mirror = lax.all_to_all(
        mirror_pieces(lookup, row, spread),
        ("ka", "vert"),
        split_axis=0,
        concat_axis=0,
        tiled=True,
        axis_index_groups=pairs,
    )
    chosen = factor_pieces(lookup, spread)
    mirror, own, chosen = lax.optimization_barrier((mirror, own, chosen))

    other = exchange(chosen, "ka")
    mirror = jnp.transpose(mirror.reshape(2, 64, 2, 4, 128), (2, 0, 1, 3, 4))
    blocks = turned(jnp.concatenate([own, mirror.reshape(2, 2, 16, 16, 128)]))

    tilde, left = spin_adapted(place, factors[:, 0], blocks)
    partial = ladder(tilde, left, other)

    groups = [[0, 2, 4, 6], [1, 3, 5, 7]]
    pieces = lax.all_to_all(
        partial, "vert", split_axis=0, concat_axis=0, tiled=True, axis_index_groups=groups
    )
    total = jnp.sum(pieces.astype(jnp.float32), 0).reshape(2, 4, 2, 2, 16, 128)
    keep = jnp.where(high == 0, total[:, :, :, 0], total[:, :, :, 1])
    give = jnp.where(high == 0, total[:, :, :, 1], total[:, :, :, 0]).astype(jnp.bfloat16)
    taken = swapped(give)
    total = (keep + taken.astype(jnp.float32)).astype(jnp.bfloat16)
    return total[:, None]


def solution(mesh):
    in_specs = (
        P(None, "ka", None, None, "vert", None),
        P(None, "ka", None, "vert", None, None),
        P(),
        P(),
        P(),
    )
    out_specs = P(None, "ka", None, None, "vert", None)
    return jax.shard_map(
        per_device, mesh=mesh, in_specs=in_specs, out_specs=out_specs, check_vma=False
    )
```

```python
import jax
import jax.numpy as jnp
from jax import lax
from jax.experimental import pallas as pl
from jax.experimental.pallas import tpu as pltpu
from jax.sharding import PartitionSpec as P

SMEM = pl.BlockSpec(memory_space=pltpu.SMEM)
VMEM = pl.BlockSpec(memory_space=pltpu.VMEM)
ANY = pl.BlockSpec(memory_space=pl.ANY)


def params(mebibytes):
    return pltpu.CompilerParams(vmem_limit_bytes=mebibytes * 1024 * 1024)


def wide(value):
    return value.astype(jnp.float32)


def exchange(value):
    return lax.all_to_all(value, "ka", split_axis=0, concat_axis=0, tiled=True)


def exchange_both(value):
    groups = [[k * 8 + 2 * y + h for h in range(2) for k in range(64)] for y in range(4)]
    return lax.all_to_all(
        value, ("ka", "vert"), split_axis=0, concat_axis=0, tiled=True, axis_index_groups=groups
    )


def mirror_kernel(kminus_ref, rows_ref, shift_ref, row_ref, spread_ref, out_ref):
    target = kminus_ref[rows_ref[row_ref[0]], shift_ref[0]]
    before = spread_ref[kminus_ref[target, 63], 6]
    for k in range(64):
        piece = spread_ref[kminus_ref[target, k], 6]
        for high in range(2):
            out_ref[high * 64 + k, 0] = piece
            out_ref[high * 64 + k, 1] = before
        before = piece


def mirror_pieces(lookup, row, spread):
    return pl.pallas_call(
        mirror_kernel,
        out_shape=jax.ShapeDtypeStruct((128, 2, 4, 128), jnp.bfloat16),
        in_specs=[SMEM] * 4 + [VMEM],
        out_specs=VMEM,
        compiler_params=params(12),
        cost_estimate=pl.CostEstimate(flops=0, bytes_accessed=700000, transcendentals=0),
        name="mirror_pieces",
    )(*lookup, row, spread)


def factor_kernel(kminus_ref, rows_ref, shift_ref, spread_ref, out_ref):
    for row in range(2):
        target = kminus_ref[rows_ref[row], shift_ref[0]]
        for k in range(64):
            out_ref[k, row * 6 : row * 6 + 6] = spread_ref[kminus_ref[target, k], 0:6]


def factor_pieces(lookup, spread):
    return pl.pallas_call(
        factor_kernel,
        out_shape=jax.ShapeDtypeStruct((64, 12, 4, 128), jnp.bfloat16),
        in_specs=[SMEM] * 3 + [VMEM],
        out_specs=VMEM,
        compiler_params=params(12),
        cost_estimate=pl.CostEstimate(flops=0, bytes_accessed=1300000, transcendentals=0),
        name="factor_pieces",
    )(*lookup, spread)


def complex_matrix(real, imag):
    return jnp.concatenate(
        [jnp.concatenate([real, -imag], 1), jnp.concatenate([imag, real], 1)], 0
    )


def ladder_kernel(place_ref, *refs):
    turns = refs[0:4]
    factor_ref, other_ref, out_ref, blocks, left, right, inner, arrived = refs[4:12]
    copies = []
    for turn in range(4):
        for high in range(2):
            start = pl.multiple_of(place_ref[turn] + high * 16, 16)
            copies.append(
                pltpu.make_async_copy(
                    turns[turn].at[:, high],
                    blocks.at[:, :, pl.ds(start, 16), :],
                    arrived.at[turn * 2 + high],
                )
            )
    for copy in copies:
        copy.start()
    for step in range(2):
        for lane in range(3):
            at = (step * 3 + lane) * 256
            left[:, at : at + 256] = complex_matrix(
                factor_ref[step, 0, lane], factor_ref[step, 1, lane]
            )
    for copy in copies:
        copy.wait()
    for row in range(2):
        other = jnp.concatenate(
            [wide(other_ref[m])[row * 24 : (row + 1) * 24] for m in range(64)], 0
        ).astype(jnp.bfloat16)
        for step in range(2):
            for lane in range(3):
                real = (step * 6 + lane) * 128
                imag = real + 384
                right[lane * 256 : (lane + 1) * 256, :] = complex_matrix(
                    other[real : real + 128], other[imag : imag + 128]
                )
            tilde = []
            for occ in range(4):
                parts = []
                for part in range(2):
                    block = (row * 4 + occ) * 2 + part
                    flipped = jnp.transpose(wide(blocks[2 + step, block]))
                    value = 2.0 * wide(blocks[step, block]) - flipped
                    parts.append(value.astype(jnp.bfloat16))
                tilde.append(jnp.concatenate(parts, 1))
            product = lax.dot_general(
                jnp.concatenate(tilde, 0),
                right[...],
                (((1,), (1,)), ((), ())),
                preferred_element_type=jnp.float32,
            ).astype(jnp.bfloat16)
            for lane in range(3):
                for part in range(2):
                    at = (step * 3 + lane) * 256 + part * 128
                    column = lane * 256 + part * 128
                    for occ in range(4):
                        inner[at : at + 128, occ * 128 : (occ + 1) * 128] = product[
                            occ * 128 : (occ + 1) * 128, column : column + 128
                        ]
        total = jnp.dot(left[...], inner[...], preferred_element_type=jnp.float32)
        total = total.astype(jnp.bfloat16)
        for occ in range(4):
            for part in range(2):
                for place in range(4):
                    at = part * 128 + place * 32
                    out_ref[place, row, occ, part] = total[
                        at : at + 32, occ * 128 : (occ + 1) * 128
                    ]


def ladder(place, turns, factor, other):
    return pl.pallas_call(
        ladder_kernel,
        out_shape=jax.ShapeDtypeStruct((4, 2, 4, 2, 32, 128), jnp.bfloat16),
        in_specs=[SMEM] + [ANY] * 4 + [VMEM, VMEM],
        out_specs=VMEM,
        scratch_shapes=[
            pltpu.VMEM((4, 16, 128, 128), jnp.bfloat16),
            pltpu.VMEM((256, 1536), jnp.bfloat16),
            pltpu.VMEM((768, 256), jnp.bfloat16),
            pltpu.VMEM((1536, 512), jnp.bfloat16),
            pltpu.SemaphoreType.DMA((8,)),
        ],
        compiler_params=params(16),
        cost_estimate=pl.CostEstimate(
            flops=1610612736, bytes_accessed=4000000, transcendentals=0
        ),
        name="ladder",
    )(place, *turns, factor, other)


def turned(value):
    return [value] + [
        lax.ppermute(value, "vert", [(v, (v + 2 * turn) % 8) for v in range(8)])
        for turn in range(1, 4)
    ]


def swapped(value):
    return lax.ppermute(value, "vert", [(v, v ^ 1) for v in range(8)])


def ahead(value):
    return lax.ppermute(value, "ka", [(k, (k + 1) % 64) for k in range(64)])


def per_device(amplitudes, factors, kminus, kj_rows, kshift):
    vert = lax.axis_index("vert")
    high = lax.rem(vert, 2)
    level = lax.div(vert, 2)
    lookup = (kminus, kj_rows, kshift)
    place = jnp.stack([lax.rem(level + 4 - turn, 4) * 32 for turn in range(4)]).astype(jnp.int32)

    row = lax.div(lax.axis_index("ka"), 32).astype(jnp.int32).reshape(1)

    shard = amplitudes[:, 0]
    spread = exchange(
        jnp.concatenate([factors[:, 0].reshape(64, 6, 4, 128), shard.reshape(64, 1, 4, 128)], 1)
    )
    behind = ahead(shard)
    other_half = swapped(shard)
    spread, behind, other_half = lax.optimization_barrier((spread, behind, other_half))

    mirror = exchange_both(mirror_pieces(lookup, row, spread))
    here = jnp.stack([shard, behind]).reshape(2, 16, 16, 128)
    there = jnp.stack([other_half, ahead(other_half)]).reshape(2, 16, 16, 128)
    own = jnp.where(
        high == 0, jnp.stack([here, there], axis=1), jnp.stack([there, here], axis=1)
    )
    chosen = factor_pieces(lookup, spread)
    mirror, own, chosen = lax.optimization_barrier((mirror, own, chosen))

    other = exchange(chosen.reshape(64, 48, 128))
    mirror = jnp.transpose(mirror.reshape(2, 64, 2, 4, 128), (2, 0, 1, 3, 4))
    turns = turned(jnp.concatenate([own, mirror.reshape(2, 2, 16, 16, 128)]))
    partial = ladder(place, turns, factors[:, 0], other)

    groups = [[0, 2, 4, 6], [1, 3, 5, 7]]
    pieces = lax.all_to_all(
        partial, "vert", split_axis=0, concat_axis=0, tiled=True, axis_index_groups=groups
    )
    total = jnp.sum(pieces.astype(jnp.float32), 0).reshape(2, 4, 2, 2, 16, 128)
    keep = jnp.where(high == 0, total[:, :, :, 0], total[:, :, :, 1])
    give = jnp.where(high == 0, total[:, :, :, 1], total[:, :, :, 0]).astype(jnp.bfloat16)
    taken = swapped(give)
    total = (keep + taken.astype(jnp.float32)).astype(jnp.bfloat16)
    return total[:, None]


def solution(mesh):
    in_specs = (
        P(None, "ka", None, None, "vert", None),
        P(None, "ka", None, "vert", None, None),
        P(),
        P(),
        P(),
    )
    out_specs = P(None, "ka", None, None, "vert", None)
    return jax.shard_map(
        per_device, mesh=mesh, in_specs=in_specs, out_specs=out_specs, check_vma=False
    )
```

```python
import jax
import jax.numpy as jnp
from jax import lax
from jax.experimental import pallas as pl
from jax.experimental.pallas import tpu as pltpu
from jax.sharding import PartitionSpec as P

SMEM = pl.BlockSpec(memory_space=pltpu.SMEM)
VMEM = pl.BlockSpec(memory_space=pltpu.VMEM)
ANY = pl.BlockSpec(memory_space=pl.ANY)


def params(mebibytes):
    return pltpu.CompilerParams(vmem_limit_bytes=mebibytes * 1024 * 1024)


def wide(value):
    return value.astype(jnp.float32)


def exchange(value):
    return lax.all_to_all(value, "ka", split_axis=0, concat_axis=0, tiled=True)


def exchange_both(value):
    groups = [[k * 8 + 2 * y + h for h in range(2) for k in range(64)] for y in range(4)]
    return lax.all_to_all(
        value, ("ka", "vert"), split_axis=0, concat_axis=0, tiled=True, axis_index_groups=groups
    )


def join_kernel(now_ref, before_ref, out_ref, done):
    copies = [
        pltpu.make_async_copy(ref, out_ref.at[:, step], done.at[step])
        for step, ref in enumerate((now_ref, before_ref))
    ]
    for copy in copies:
        copy.start()
    for copy in copies:
        copy.wait()


def joined(now, before):
    return pl.pallas_call(
        join_kernel,
        out_shape=jax.ShapeDtypeStruct((2, 2, 2, 16, 16, 128), jnp.bfloat16),
        in_specs=[ANY, ANY],
        out_specs=VMEM,
        scratch_shapes=[pltpu.SemaphoreType.DMA((2,))],
        compiler_params=params(8),
        cost_estimate=pl.CostEstimate(flops=115000000000, bytes_accessed=1000000, transcendentals=0),
        name="joined",
    )(now, before)


def mirror_kernel(kminus_ref, rows_ref, shift_ref, row_ref, spread_ref, out_ref):
    target = kminus_ref[rows_ref[row_ref[0]], shift_ref[0]]
    for k in range(64):
        piece = spread_ref[kminus_ref[target, k], 6]
        out_ref[k] = piece
        out_ref[64 + k] = piece


def mirror_pieces(lookup, row, spread):
    return pl.pallas_call(
        mirror_kernel,
        out_shape=jax.ShapeDtypeStruct((128, 4, 128), jnp.bfloat16),
        in_specs=[SMEM] * 4 + [VMEM],
        out_specs=VMEM,
        compiler_params=params(12),
        cost_estimate=pl.CostEstimate(flops=0, bytes_accessed=700000, transcendentals=0),
        name="mirror_pieces",
    )(*lookup, row, spread)


def factor_kernel(kminus_ref, rows_ref, shift_ref, spread_ref, out_ref):
    for row in range(2):
        target = kminus_ref[rows_ref[row], shift_ref[0]]
        for k in range(64):
            out_ref[k, row * 6 : row * 6 + 6] = spread_ref[kminus_ref[target, k], 0:6]


def factor_pieces(lookup, spread):
    return pl.pallas_call(
        factor_kernel,
        out_shape=jax.ShapeDtypeStruct((64, 12, 4, 128), jnp.bfloat16),
        in_specs=[SMEM] * 3 + [VMEM],
        out_specs=VMEM,
        compiler_params=params(12),
        cost_estimate=pl.CostEstimate(flops=0, bytes_accessed=1300000, transcendentals=0),
        name="factor_pieces",
    )(*lookup, spread)


def complex_matrix(real, imag):
    return jnp.concatenate(
        [jnp.concatenate([real, -imag], 1), jnp.concatenate([imag, real], 1)], 0
    )


def ladder_kernel(place_ref, *refs):
    turns = refs[0:4]
    factor_ref, other_ref, out_ref, blocks, left, right, inner, arrived = refs[4:12]
    copies = []
    for turn in range(4):
        for high in range(2):
            start = pl.multiple_of(place_ref[turn] + high * 16, 16)
            copies.append(
                pltpu.make_async_copy(
                    turns[turn].at[:, high],
                    blocks.at[:, :, pl.ds(start, 16), :],
                    arrived.at[turn * 2 + high],
                )
            )
    for copy in copies:
        copy.start()
    for step in range(2):
        for lane in range(3):
            at = (step * 3 + lane) * 256
            left[:, at : at + 256] = complex_matrix(
                factor_ref[step, 0, lane], factor_ref[step, 1, lane]
            )
    for copy in copies:
        copy.wait()
    for row in range(2):
        other = jnp.concatenate(
            [wide(other_ref[m])[row * 24 : (row + 1) * 24] for m in range(64)], 0
        ).astype(jnp.bfloat16)
        for step in range(2):
            for lane in range(3):
                real = (step * 6 + lane) * 128
                imag = real + 384
                right[lane * 256 : (lane + 1) * 256, :] = complex_matrix(
                    other[real : real + 128], other[imag : imag + 128]
                )
            tilde = []
            for occ in range(4):
                parts = []
                for part in range(2):
                    block = (row * 4 + occ) * 2 + part
                    flipped = jnp.transpose(wide(blocks[2 + step, block]))
                    value = 2.0 * wide(blocks[step, block]) - flipped
                    parts.append(value.astype(jnp.bfloat16))
                tilde.append(jnp.concatenate(parts, 1))
            product = lax.dot_general(
                jnp.concatenate(tilde, 0),
                right[...],
                (((1,), (1,)), ((), ())),
                preferred_element_type=jnp.float32,
            ).astype(jnp.bfloat16)
            for lane in range(3):
                for part in range(2):
                    at = (step * 3 + lane) * 256 + part * 128
                    column = lane * 256 + part * 128
                    for occ in range(4):
                        inner[at : at + 128, occ * 128 : (occ + 1) * 128] = product[
                            occ * 128 : (occ + 1) * 128, column : column + 128
                        ]
        total = jnp.dot(left[...], inner[...], preferred_element_type=jnp.float32)
        total = total.astype(jnp.bfloat16)
        for occ in range(4):
            for part in range(2):
                for place in range(4):
                    at = part * 128 + place * 32
                    out_ref[place, row, occ, part] = total[
                        at : at + 32, occ * 128 : (occ + 1) * 128
                    ]


def ladder(place, turns, factor, other):
    return pl.pallas_call(
        ladder_kernel,
        out_shape=jax.ShapeDtypeStruct((4, 2, 4, 2, 32, 128), jnp.bfloat16),
        in_specs=[SMEM] + [ANY] * 4 + [VMEM, VMEM],
        out_specs=VMEM,
        scratch_shapes=[
            pltpu.VMEM((4, 16, 128, 128), jnp.bfloat16),
            pltpu.VMEM((256, 1536), jnp.bfloat16),
            pltpu.VMEM((768, 256), jnp.bfloat16),
            pltpu.VMEM((1536, 512), jnp.bfloat16),
            pltpu.SemaphoreType.DMA((8,)),
        ],
        compiler_params=params(16),
        cost_estimate=pl.CostEstimate(
            flops=1610612736, bytes_accessed=4000000, transcendentals=0
        ),
        name="ladder",
    )(place, *turns, factor, other)


def turned(value):
    return [value] + [
        lax.ppermute(value, "vert", [(v, (v + 2 * turn) % 8) for v in range(8)])
        for turn in range(1, 4)
    ]


def swapped(value):
    return lax.ppermute(value, "vert", [(v, v ^ 1) for v in range(8)])


def ahead(value):
    pairs = [
        (k * 8 + v, (k + 1) * 8 + v if k < 63 else v ^ 1) for k in range(64) for v in range(8)
    ]
    return lax.ppermute(value, ("ka", "vert"), pairs)


def per_device(amplitudes, factors, kminus, kj_rows, kshift):
    vert = lax.axis_index("vert")
    high = lax.rem(vert, 2)
    level = lax.div(vert, 2)
    lookup = (kminus, kj_rows, kshift)
    place = jnp.stack([lax.rem(level + 4 - turn, 4) * 32 for turn in range(4)]).astype(jnp.int32)

    row = lax.div(lax.axis_index("ka"), 32).astype(jnp.int32).reshape(1)

    shard = amplitudes[:, 0]
    spread = exchange(
        jnp.concatenate([factors[:, 0].reshape(64, 6, 4, 128), shard.reshape(64, 1, 4, 128)], 1)
    )
    other_half = swapped(shard)
    spread, other_half = lax.optimization_barrier((spread, other_half))

    mirror = exchange_both(mirror_pieces(lookup, row, spread))
    own = jnp.where(
        high == 0, jnp.stack([shard, other_half]), jnp.stack([other_half, shard])
    )
    chosen = factor_pieces(lookup, spread)
    mirror, own, chosen = lax.optimization_barrier((mirror, own, chosen))

    other = exchange(chosen.reshape(64, 48, 128))
    now = jnp.stack([own.reshape(2, 16, 16, 128), mirror.reshape(2, 16, 16, 128)])
    turns = turned(joined(now, ahead(now)).reshape(4, 2, 16, 16, 128))
    partial = ladder(place, turns, factors[:, 0], other)

    groups = [[0, 2, 4, 6], [1, 3, 5, 7]]
    pieces = lax.all_to_all(
        partial, "vert", split_axis=0, concat_axis=0, tiled=True, axis_index_groups=groups
    )
    total = jnp.sum(pieces.astype(jnp.float32), 0).reshape(2, 4, 2, 2, 16, 128)
    keep = jnp.where(high == 0, total[:, :, :, 0], total[:, :, :, 1])
    give = jnp.where(high == 0, total[:, :, :, 1], total[:, :, :, 0]).astype(jnp.bfloat16)
    taken = swapped(give)
    total = (keep + taken.astype(jnp.float32)).astype(jnp.bfloat16)
    return total[:, None]


def solution(mesh):
    in_specs = (
        P(None, "ka", None, None, "vert", None),
        P(None, "ka", None, "vert", None, None),
        P(),
        P(),
        P(),
    )
    out_specs = P(None, "ka", None, None, "vert", None)
    return jax.shard_map(
        per_device, mesh=mesh, in_specs=in_specs, out_specs=out_specs, check_vma=False
    )
```

```python
import jax
import jax.numpy as jnp
from jax import lax
from jax.experimental import pallas as pl
from jax.experimental.pallas import tpu as pltpu
from jax.sharding import PartitionSpec as P

SMEM = pl.BlockSpec(memory_space=pltpu.SMEM)
VMEM = pl.BlockSpec(memory_space=pltpu.VMEM)
ANY = pl.BlockSpec(memory_space=pl.ANY)


def params(mebibytes):
    return pltpu.CompilerParams(vmem_limit_bytes=mebibytes * 1024 * 1024)


def wide(value):
    return value.astype(jnp.float32)


def exchange(value):
    return lax.all_to_all(value, "ka", split_axis=0, concat_axis=0, tiled=True)


def exchange_both(value):
    groups = [[k * 8 + 2 * y + h for h in range(2) for k in range(64)] for y in range(4)]
    return lax.all_to_all(
        value, ("ka", "vert"), split_axis=0, concat_axis=0, tiled=True, axis_index_groups=groups
    )


def join_kernel(high_ref, here_ref, there_ref, now_ref, before_ref, out_ref, done):
    high = high_ref[0]
    copies = [
        pltpu.make_async_copy(here_ref, out_ref.at[pl.ds(0, 2), high], done.at[0]),
        pltpu.make_async_copy(there_ref, out_ref.at[pl.ds(0, 2), 1 - high], done.at[1]),
        pltpu.make_async_copy(now_ref, out_ref.at[2], done.at[2]),
        pltpu.make_async_copy(before_ref, out_ref.at[3], done.at[3]),
    ]
    for copy in copies:
        copy.start()
    for copy in copies:
        copy.wait()


def joined(high, *parts):
    return pl.pallas_call(
        join_kernel,
        out_shape=jax.ShapeDtypeStruct((4, 2, 16, 16, 128), jnp.bfloat16),
        in_specs=[SMEM] + [ANY] * 4,
        out_specs=VMEM,
        scratch_shapes=[pltpu.SemaphoreType.DMA((4,))],
        compiler_params=params(8),
        cost_estimate=pl.CostEstimate(
            flops=115000000000, bytes_accessed=1000000, transcendentals=0
        ),
        name="joined",
    )(high, *parts)


def mirror_kernel(kminus_ref, rows_ref, shift_ref, row_ref, spread_ref, out_ref):
    target = kminus_ref[rows_ref[row_ref[0]], shift_ref[0]]
    for k in range(64):
        piece = spread_ref[kminus_ref[target, k], 6]
        out_ref[k] = piece
        out_ref[64 + k] = piece


def mirror_pieces(lookup, row, spread):
    return pl.pallas_call(
        mirror_kernel,
        out_shape=jax.ShapeDtypeStruct((128, 4, 128), jnp.bfloat16),
        in_specs=[SMEM] * 4 + [VMEM],
        out_specs=VMEM,
        compiler_params=params(12),
        cost_estimate=pl.CostEstimate(flops=0, bytes_accessed=700000, transcendentals=0),
        name="mirror_pieces",
    )(*lookup, row, spread)


def factor_kernel(kminus_ref, rows_ref, shift_ref, spread_ref, out_ref):
    for row in range(2):
        target = kminus_ref[rows_ref[row], shift_ref[0]]
        for k in range(64):
            out_ref[k, row * 6 : row * 6 + 6] = spread_ref[kminus_ref[target, k], 0:6]


def factor_pieces(lookup, spread):
    return pl.pallas_call(
        factor_kernel,
        out_shape=jax.ShapeDtypeStruct((64, 12, 4, 128), jnp.bfloat16),
        in_specs=[SMEM] * 3 + [VMEM],
        out_specs=VMEM,
        compiler_params=params(12),
        cost_estimate=pl.CostEstimate(flops=0, bytes_accessed=1300000, transcendentals=0),
        name="factor_pieces",
    )(*lookup, spread)


def complex_matrix(real, imag):
    return jnp.concatenate(
        [jnp.concatenate([real, -imag], 1), jnp.concatenate([imag, real], 1)], 0
    )


def ladder_kernel(place_ref, *refs):
    turns = refs[0:4]
    factor_ref, other_ref, out_ref, blocks, left, right, inner, arrived = refs[4:12]
    copies = []
    for turn in range(4):
        for high in range(2):
            start = pl.multiple_of(place_ref[turn] + high * 16, 16)
            copies.append(
                pltpu.make_async_copy(
                    turns[turn].at[:, high],
                    blocks.at[:, :, pl.ds(start, 16), :],
                    arrived.at[turn * 2 + high],
                )
            )
    for copy in copies:
        copy.start()
    for step in range(2):
        for lane in range(3):
            at = (step * 3 + lane) * 256
            left[:, at : at + 256] = complex_matrix(
                factor_ref[step, 0, lane], factor_ref[step, 1, lane]
            )
    for copy in copies:
        copy.wait()
    for row in range(2):
        other = jnp.concatenate(
            [wide(other_ref[m])[row * 24 : (row + 1) * 24] for m in range(64)], 0
        ).astype(jnp.bfloat16)
        for step in range(2):
            for lane in range(3):
                real = (step * 6 + lane) * 128
                imag = real + 384
                right[lane * 256 : (lane + 1) * 256, :] = complex_matrix(
                    other[real : real + 128], other[imag : imag + 128]
                )
            tilde = []
            for occ in range(4):
                parts = []
                for part in range(2):
                    block = (row * 4 + occ) * 2 + part
                    flipped = jnp.transpose(wide(blocks[2 + step, block]))
                    value = 2.0 * wide(blocks[step, block]) - flipped
                    parts.append(value.astype(jnp.bfloat16))
                tilde.append(jnp.concatenate(parts, 1))
            product = lax.dot_general(
                jnp.concatenate(tilde, 0),
                right[...],
                (((1,), (1,)), ((), ())),
                preferred_element_type=jnp.float32,
            ).astype(jnp.bfloat16)
            for lane in range(3):
                for part in range(2):
                    at = (step * 3 + lane) * 256 + part * 128
                    column = lane * 256 + part * 128
                    for occ in range(4):
                        inner[at : at + 128, occ * 128 : (occ + 1) * 128] = product[
                            occ * 128 : (occ + 1) * 128, column : column + 128
                        ]
        total = jnp.dot(left[...], inner[...], preferred_element_type=jnp.float32)
        total = total.astype(jnp.bfloat16)
        for occ in range(4):
            for part in range(2):
                for place in range(4):
                    at = part * 128 + place * 32
                    out_ref[place, row, occ, part] = total[
                        at : at + 32, occ * 128 : (occ + 1) * 128
                    ]


def ladder(place, turns, factor, other):
    return pl.pallas_call(
        ladder_kernel,
        out_shape=jax.ShapeDtypeStruct((4, 2, 4, 2, 32, 128), jnp.bfloat16),
        in_specs=[SMEM] + [ANY] * 4 + [VMEM, VMEM],
        out_specs=VMEM,
        scratch_shapes=[
            pltpu.VMEM((4, 16, 128, 128), jnp.bfloat16),
            pltpu.VMEM((256, 1536), jnp.bfloat16),
            pltpu.VMEM((768, 256), jnp.bfloat16),
            pltpu.VMEM((1536, 512), jnp.bfloat16),
            pltpu.SemaphoreType.DMA((8,)),
        ],
        compiler_params=params(16),
        cost_estimate=pl.CostEstimate(
            flops=1610612736, bytes_accessed=4000000, transcendentals=0
        ),
        name="ladder",
    )(place, *turns, factor, other)


def turned(value):
    return [value] + [
        lax.ppermute(value, "vert", [(v, (v + 2 * turn) % 8) for v in range(8)])
        for turn in range(1, 4)
    ]


def swapped(value):
    return lax.ppermute(value, "vert", [(v, v ^ 1) for v in range(8)])


def passed(value):
    return lax.ppermute(value, "ka", [(k, (k + 1) % 64) for k in range(64)])


def ahead(value):
    pairs = [
        (k * 8 + v, (k + 1) * 8 + v if k < 63 else v ^ 1) for k in range(64) for v in range(8)
    ]
    return lax.ppermute(value, ("ka", "vert"), pairs)


def per_device(amplitudes, factors, kminus, kj_rows, kshift):
    vert = lax.axis_index("vert")
    high = lax.rem(vert, 2)
    level = lax.div(vert, 2)
    lookup = (kminus, kj_rows, kshift)
    place = jnp.stack([lax.rem(level + 4 - turn, 4) * 32 for turn in range(4)]).astype(jnp.int32)

    row = lax.div(lax.axis_index("ka"), 32).astype(jnp.int32).reshape(1)

    shard = amplitudes[:, 0]
    spread = exchange(
        jnp.concatenate([factors[:, 0].reshape(64, 6, 4, 128), shard.reshape(64, 1, 4, 128)], 1)
    )
    behind = passed(shard)
    spread, behind = lax.optimization_barrier((spread, behind))

    mirror = exchange_both(mirror_pieces(lookup, row, spread))
    here = jnp.stack([shard, behind]).reshape(2, 16, 16, 128)
    chosen = factor_pieces(lookup, spread)
    here, chosen = lax.optimization_barrier((here, chosen))
    there = swapped(here)
    mirror, chosen = lax.optimization_barrier((mirror, chosen))

    other = exchange(chosen.reshape(64, 48, 128))
    mirror = mirror.reshape(2, 16, 16, 128)
    turns = turned(
        joined(high.astype(jnp.int32).reshape(1), here, there, mirror, ahead(mirror))
    )
    partial = ladder(place, turns, factors[:, 0], other)

    groups = [[0, 2, 4, 6], [1, 3, 5, 7]]
    pieces = lax.all_to_all(
        partial, "vert", split_axis=0, concat_axis=0, tiled=True, axis_index_groups=groups
    )
    total = jnp.sum(pieces.astype(jnp.float32), 0).reshape(2, 4, 2, 2, 16, 128)
    keep = jnp.where(high == 0, total[:, :, :, 0], total[:, :, :, 1])
    give = jnp.where(high == 0, total[:, :, :, 1], total[:, :, :, 0]).astype(jnp.bfloat16)
    taken = swapped(give)
    total = (keep + taken.astype(jnp.float32)).astype(jnp.bfloat16)
    return total[:, None]


def solution(mesh):
    in_specs = (
        P(None, "ka", None, None, "vert", None),
        P(None, "ka", None, "vert", None, None),
        P(),
        P(),
        P(),
    )
    out_specs = P(None, "ka", None, None, "vert", None)
    return jax.shard_map(
        per_device, mesh=mesh, in_specs=in_specs, out_specs=out_specs, check_vma=False
    )
```

```python
import jax
import jax.numpy as jnp
from jax import lax
from jax.experimental import pallas as pl
from jax.experimental.pallas import tpu as pltpu
from jax.sharding import PartitionSpec as P

ORDER = [
    36, 0, 50, 59, 23, 52, 35, 28, 53, 32, 1, 30, 46, 27, 9, 10,
    13, 60, 29, 54, 17, 62, 44, 57, 12, 14, 61, 16, 2, 25, 19, 48,
    6, 55, 24, 5, 42, 33, 41, 58, 4, 38, 3, 39, 37, 20, 26, 51,
    47, 21, 56, 31, 49, 34, 7, 63, 11, 18, 43, 22, 8, 45, 15, 40,
]
RANK = [ORDER.index(k) for k in range(64)]

SMEM = pl.BlockSpec(memory_space=pltpu.SMEM)
VMEM = pl.BlockSpec(memory_space=pltpu.VMEM)
ANY = pl.BlockSpec(memory_space=pl.ANY)


def params(mebibytes):
    return pltpu.CompilerParams(vmem_limit_bytes=mebibytes * 1024 * 1024)


def wide(value):
    return value.astype(jnp.float32)


def exchange(value):
    return lax.all_to_all(
        value, "ka", split_axis=0, concat_axis=0, tiled=True, axis_index_groups=[ORDER]
    )


def exchange_both(value):
    groups = [[k * 8 + 2 * y + h for h in range(2) for k in ORDER] for y in range(4)]
    return lax.all_to_all(
        value, ("ka", "vert"), split_axis=0, concat_axis=0, tiled=True, axis_index_groups=groups
    )


def join_kernel(high_ref, here_ref, there_ref, now_ref, before_ref, out_ref, done):
    high = high_ref[0]
    copies = [
        pltpu.make_async_copy(here_ref, out_ref.at[pl.ds(0, 2), high], done.at[0]),
        pltpu.make_async_copy(there_ref, out_ref.at[pl.ds(0, 2), 1 - high], done.at[1]),
        pltpu.make_async_copy(now_ref, out_ref.at[2], done.at[2]),
        pltpu.make_async_copy(before_ref, out_ref.at[3], done.at[3]),
    ]
    for copy in copies:
        copy.start()
    for copy in copies:
        copy.wait()


def joined(high, *parts):
    return pl.pallas_call(
        join_kernel,
        out_shape=jax.ShapeDtypeStruct((4, 2, 16, 16, 128), jnp.bfloat16),
        in_specs=[SMEM] + [ANY] * 4,
        out_specs=VMEM,
        scratch_shapes=[pltpu.SemaphoreType.DMA((4,))],
        compiler_params=params(8),
        cost_estimate=pl.CostEstimate(
            flops=115000000000, bytes_accessed=1000000, transcendentals=0
        ),
        name="joined",
    )(high, *parts)


def mirror_kernel(rank_ref, kminus_ref, rows_ref, shift_ref, row_ref, spread_ref, out_ref):
    target = kminus_ref[rows_ref[row_ref[0]], shift_ref[0]]
    for at, k in enumerate(ORDER):
        piece = spread_ref[rank_ref[kminus_ref[target, k]], 6]
        out_ref[at] = piece
        out_ref[64 + at] = piece


def mirror_pieces(lookup, row, spread):
    return pl.pallas_call(
        mirror_kernel,
        out_shape=jax.ShapeDtypeStruct((128, 4, 128), jnp.bfloat16),
        in_specs=[SMEM] * 5 + [VMEM],
        out_specs=VMEM,
        compiler_params=params(12),
        cost_estimate=pl.CostEstimate(flops=0, bytes_accessed=700000, transcendentals=0),
        name="mirror_pieces",
    )(*lookup, row, spread)


def factor_kernel(rank_ref, kminus_ref, rows_ref, shift_ref, spread_ref, out_ref):
    for row in range(2):
        target = kminus_ref[rows_ref[row], shift_ref[0]]
        for at, k in enumerate(ORDER):
            out_ref[at, row * 6 : row * 6 + 6] = spread_ref[
                rank_ref[kminus_ref[target, k]], 0:6
            ]


def factor_pieces(lookup, spread):
    return pl.pallas_call(
        factor_kernel,
        out_shape=jax.ShapeDtypeStruct((64, 12, 4, 128), jnp.bfloat16),
        in_specs=[SMEM] * 4 + [VMEM],
        out_specs=VMEM,
        compiler_params=params(12),
        cost_estimate=pl.CostEstimate(flops=0, bytes_accessed=1300000, transcendentals=0),
        name="factor_pieces",
    )(*lookup, spread)


def complex_matrix(real, imag):
    return jnp.concatenate(
        [jnp.concatenate([real, -imag], 1), jnp.concatenate([imag, real], 1)], 0
    )


def ladder_kernel(place_ref, *refs):
    turns = refs[0:4]
    factor_ref, other_ref, out_ref, blocks, left, right, inner, arrived = refs[4:12]
    copies = []
    for turn in range(4):
        for high in range(2):
            start = pl.multiple_of(place_ref[turn] + high * 16, 16)
            copies.append(
                pltpu.make_async_copy(
                    turns[turn].at[:, high],
                    blocks.at[:, :, pl.ds(start, 16), :],
                    arrived.at[turn * 2 + high],
                )
            )
    for copy in copies:
        copy.start()
    for step in range(2):
        for lane in range(3):
            at = (step * 3 + lane) * 256
            left[:, at : at + 256] = complex_matrix(
                factor_ref[step, 0, lane], factor_ref[step, 1, lane]
            )
    for copy in copies:
        copy.wait()
    for row in range(2):
        other = jnp.concatenate(
            [wide(other_ref[m])[row * 24 : (row + 1) * 24] for m in range(64)], 0
        ).astype(jnp.bfloat16)
        for step in range(2):
            for lane in range(3):
                real = (step * 6 + lane) * 128
                imag = real + 384
                right[lane * 256 : (lane + 1) * 256, :] = complex_matrix(
                    other[real : real + 128], other[imag : imag + 128]
                )
            tilde = []
            for occ in range(4):
                parts = []
                for part in range(2):
                    block = (row * 4 + occ) * 2 + part
                    flipped = jnp.transpose(wide(blocks[2 + step, block]))
                    value = 2.0 * wide(blocks[step, block]) - flipped
                    parts.append(value.astype(jnp.bfloat16))
                tilde.append(jnp.concatenate(parts, 1))
            product = lax.dot_general(
                jnp.concatenate(tilde, 0),
                right[...],
                (((1,), (1,)), ((), ())),
                preferred_element_type=jnp.float32,
            ).astype(jnp.bfloat16)
            for lane in range(3):
                for part in range(2):
                    at = (step * 3 + lane) * 256 + part * 128
                    column = lane * 256 + part * 128
                    for occ in range(4):
                        inner[at : at + 128, occ * 128 : (occ + 1) * 128] = product[
                            occ * 128 : (occ + 1) * 128, column : column + 128
                        ]
        total = jnp.dot(left[...], inner[...], preferred_element_type=jnp.float32)
        total = total.astype(jnp.bfloat16)
        for occ in range(4):
            for part in range(2):
                for place in range(4):
                    at = part * 128 + place * 32
                    out_ref[place, row, occ, part] = total[
                        at : at + 32, occ * 128 : (occ + 1) * 128
                    ]


def ladder(place, turns, factor, other):
    return pl.pallas_call(
        ladder_kernel,
        out_shape=jax.ShapeDtypeStruct((4, 2, 4, 2, 32, 128), jnp.bfloat16),
        in_specs=[SMEM] + [ANY] * 4 + [VMEM, VMEM],
        out_specs=VMEM,
        scratch_shapes=[
            pltpu.VMEM((4, 16, 128, 128), jnp.bfloat16),
            pltpu.VMEM((256, 1536), jnp.bfloat16),
            pltpu.VMEM((768, 256), jnp.bfloat16),
            pltpu.VMEM((1536, 512), jnp.bfloat16),
            pltpu.SemaphoreType.DMA((8,)),
        ],
        compiler_params=params(16),
        cost_estimate=pl.CostEstimate(
            flops=1610612736, bytes_accessed=4000000, transcendentals=0
        ),
        name="ladder",
    )(place, *turns, factor, other)


def turned(value):
    return [value] + [
        lax.ppermute(value, "vert", [(v, (v + 2 * turn) % 8) for v in range(8)])
        for turn in range(1, 4)
    ]


def swapped(value):
    return lax.ppermute(value, "vert", [(v, v ^ 1) for v in range(8)])


def passed(value):
    return lax.ppermute(value, "ka", [(k, (k + 1) % 64) for k in range(64)])


def ahead(value):
    pairs = [
        (k * 8 + v, (k + 1) * 8 + v if k < 63 else v ^ 1) for k in range(64) for v in range(8)
    ]
    return lax.ppermute(value, ("ka", "vert"), pairs)


def per_device(amplitudes, factors, kminus, kj_rows, kshift):
    vert = lax.axis_index("vert")
    high = lax.rem(vert, 2)
    level = lax.div(vert, 2)
    rank = jnp.array(RANK, jnp.int32)
    lookup = (rank, kminus, kj_rows, kshift)
    place = jnp.stack([lax.rem(level + 4 - turn, 4) * 32 for turn in range(4)]).astype(jnp.int32)

    row = lax.div(rank[lax.axis_index("ka")], 32).reshape(1)

    shard = amplitudes[:, 0]
    spread = exchange(
        jnp.concatenate([factors[:, 0].reshape(64, 6, 4, 128), shard.reshape(64, 1, 4, 128)], 1)
    )
    behind = passed(shard)
    spread, behind = lax.optimization_barrier((spread, behind))

    mirror = exchange_both(mirror_pieces(lookup, row, spread))
    here = jnp.stack([shard, behind]).reshape(2, 16, 16, 128)
    chosen = factor_pieces(lookup, spread)
    here, chosen = lax.optimization_barrier((here, chosen))
    there = swapped(here)
    mirror, chosen = lax.optimization_barrier((mirror, chosen))

    other = exchange(chosen.reshape(64, 48, 128))
    mirror = mirror.reshape(2, 16, 16, 128)
    turns = turned(
        joined(high.astype(jnp.int32).reshape(1), here, there, mirror, ahead(mirror))
    )
    partial = ladder(place, turns, factors[:, 0], other)

    groups = [[0, 2, 4, 6], [1, 3, 5, 7]]
    pieces = lax.all_to_all(
        partial, "vert", split_axis=0, concat_axis=0, tiled=True, axis_index_groups=groups
    )
    total = jnp.sum(pieces.astype(jnp.float32), 0).reshape(2, 4, 2, 2, 16, 128)
    keep = jnp.where(high == 0, total[:, :, :, 0], total[:, :, :, 1])
    give = jnp.where(high == 0, total[:, :, :, 1], total[:, :, :, 0]).astype(jnp.bfloat16)
    taken = swapped(give)
    total = (keep + taken.astype(jnp.float32)).astype(jnp.bfloat16)
    return total[:, None]


def solution(mesh):
    in_specs = (
        P(None, "ka", None, None, "vert", None),
        P(None, "ka", None, "vert", None, None),
        P(),
        P(),
        P(),
    )
    out_specs = P(None, "ka", None, None, "vert", None)
    return jax.shard_map(
        per_device, mesh=mesh, in_specs=in_specs, out_specs=out_specs, check_vma=False
    )
```

```python
import jax
import jax.numpy as jnp
from jax import lax
from jax.experimental import pallas as pl
from jax.experimental.pallas import tpu as pltpu
from jax.sharding import PartitionSpec as P

ORDER = [
    29, 59, 17, 8, 28, 7, 44, 46, 23, 57, 24, 21, 51, 43, 47, 19,
    31, 55, 4, 1, 15, 14, 45, 37, 26, 9, 42, 62, 61, 20, 16, 38,
    54, 41, 32, 30, 33, 39, 36, 35, 53, 18, 50, 56, 40, 0, 10, 63,
    34, 25, 13, 5, 52, 60, 22, 48, 12, 58, 3, 2, 49, 6, 27, 11,
]
RANK = [ORDER.index(k) for k in range(64)]

SMEM = pl.BlockSpec(memory_space=pltpu.SMEM)
VMEM = pl.BlockSpec(memory_space=pltpu.VMEM)
ANY = pl.BlockSpec(memory_space=pl.ANY)


def params(mebibytes):
    return pltpu.CompilerParams(vmem_limit_bytes=mebibytes * 1024 * 1024)


def wide(value):
    return value.astype(jnp.float32)


def exchange(value):
    return lax.all_to_all(
        value, "ka", split_axis=0, concat_axis=0, tiled=True, axis_index_groups=[ORDER]
    )


def exchange_both(value):
    groups = [[k * 8 + 2 * y + h for h in range(2) for k in ORDER] for y in range(4)]
    return lax.all_to_all(
        value, ("ka", "vert"), split_axis=0, concat_axis=0, tiled=True, axis_index_groups=groups
    )


def join_kernel(high_ref, here_ref, there_ref, now_ref, before_ref, out_ref, done):
    high = high_ref[0]
    copies = [
        pltpu.make_async_copy(here_ref, out_ref.at[pl.ds(0, 2), high], done.at[0]),
        pltpu.make_async_copy(there_ref, out_ref.at[pl.ds(0, 2), 1 - high], done.at[1]),
        pltpu.make_async_copy(now_ref, out_ref.at[2], done.at[2]),
        pltpu.make_async_copy(before_ref, out_ref.at[3], done.at[3]),
    ]
    for copy in copies:
        copy.start()
    for copy in copies:
        copy.wait()


def joined(high, *parts):
    return pl.pallas_call(
        join_kernel,
        out_shape=jax.ShapeDtypeStruct((4, 2, 16, 16, 128), jnp.bfloat16),
        in_specs=[SMEM] + [ANY] * 4,
        out_specs=VMEM,
        scratch_shapes=[pltpu.SemaphoreType.DMA((4,))],
        compiler_params=params(8),
        cost_estimate=pl.CostEstimate(
            flops=115000000000, bytes_accessed=1000000, transcendentals=0
        ),
        name="joined",
    )(high, *parts)


def mirror_kernel(rank_ref, kminus_ref, rows_ref, shift_ref, row_ref, spread_ref, out_ref):
    target = kminus_ref[rows_ref[row_ref[0]], shift_ref[0]]
    for at, k in enumerate(ORDER):
        piece = spread_ref[rank_ref[kminus_ref[target, k]], 6]
        out_ref[at] = piece
        out_ref[64 + at] = piece


def mirror_pieces(lookup, row, spread):
    return pl.pallas_call(
        mirror_kernel,
        out_shape=jax.ShapeDtypeStruct((128, 4, 128), jnp.bfloat16),
        in_specs=[SMEM] * 5 + [VMEM],
        out_specs=VMEM,
        compiler_params=params(12),
        cost_estimate=pl.CostEstimate(flops=0, bytes_accessed=700000, transcendentals=0),
        name="mirror_pieces",
    )(*lookup, row, spread)


def factor_kernel(rank_ref, kminus_ref, rows_ref, shift_ref, spread_ref, out_ref):
    for row in range(2):
        target = kminus_ref[rows_ref[row], shift_ref[0]]
        for at, k in enumerate(ORDER):
            out_ref[at, row * 6 : row * 6 + 6] = spread_ref[
                rank_ref[kminus_ref[target, k]], 0:6
            ]


def factor_pieces(lookup, spread):
    return pl.pallas_call(
        factor_kernel,
        out_shape=jax.ShapeDtypeStruct((64, 12, 4, 128), jnp.bfloat16),
        in_specs=[SMEM] * 4 + [VMEM],
        out_specs=VMEM,
        compiler_params=params(12),
        cost_estimate=pl.CostEstimate(flops=0, bytes_accessed=1300000, transcendentals=0),
        name="factor_pieces",
    )(*lookup, spread)


def complex_matrix(real, imag):
    return jnp.concatenate(
        [jnp.concatenate([real, -imag], 1), jnp.concatenate([imag, real], 1)], 0
    )


def ladder_kernel(place_ref, *refs):
    turns = refs[0:4]
    factor_ref, other_ref, out_ref, blocks, left, right, inner, arrived = refs[4:12]
    copies = []
    for turn in range(4):
        for high in range(2):
            start = pl.multiple_of(place_ref[turn] + high * 16, 16)
            copies.append(
                pltpu.make_async_copy(
                    turns[turn].at[:, high],
                    blocks.at[:, :, pl.ds(start, 16), :],
                    arrived.at[turn * 2 + high],
                )
            )
    for copy in copies:
        copy.start()
    for step in range(2):
        for lane in range(3):
            at = (step * 3 + lane) * 256
            left[:, at : at + 256] = complex_matrix(
                factor_ref[step, 0, lane], factor_ref[step, 1, lane]
            )
    for copy in copies:
        copy.wait()
    for row in range(2):
        other = jnp.concatenate(
            [wide(other_ref[m])[row * 24 : (row + 1) * 24] for m in range(64)], 0
        ).astype(jnp.bfloat16)
        for step in range(2):
            for lane in range(3):
                real = (step * 6 + lane) * 128
                imag = real + 384
                right[lane * 256 : (lane + 1) * 256, :] = complex_matrix(
                    other[real : real + 128], other[imag : imag + 128]
                )
            tilde = []
            for occ in range(4):
                parts = []
                for part in range(2):
                    block = (row * 4 + occ) * 2 + part
                    flipped = jnp.transpose(wide(blocks[2 + step, block]))
                    value = 2.0 * wide(blocks[step, block]) - flipped
                    parts.append(value.astype(jnp.bfloat16))
                tilde.append(jnp.concatenate(parts, 1))
            product = lax.dot_general(
                jnp.concatenate(tilde, 0),
                right[...],
                (((1,), (1,)), ((), ())),
                preferred_element_type=jnp.float32,
            ).astype(jnp.bfloat16)
            for lane in range(3):
                for part in range(2):
                    at = (step * 3 + lane) * 256 + part * 128
                    column = lane * 256 + part * 128
                    for occ in range(4):
                        inner[at : at + 128, occ * 128 : (occ + 1) * 128] = product[
                            occ * 128 : (occ + 1) * 128, column : column + 128
                        ]
        total = jnp.dot(left[...], inner[...], preferred_element_type=jnp.float32)
        total = total.astype(jnp.bfloat16)
        for occ in range(4):
            for part in range(2):
                for place in range(4):
                    at = part * 128 + place * 32
                    out_ref[place, row, occ, part] = total[
                        at : at + 32, occ * 128 : (occ + 1) * 128
                    ]


def ladder(place, turns, factor, other):
    return pl.pallas_call(
        ladder_kernel,
        out_shape=jax.ShapeDtypeStruct((4, 2, 4, 2, 32, 128), jnp.bfloat16),
        in_specs=[SMEM] + [ANY] * 4 + [VMEM, VMEM],
        out_specs=VMEM,
        scratch_shapes=[
            pltpu.VMEM((4, 16, 128, 128), jnp.bfloat16),
            pltpu.VMEM((256, 1536), jnp.bfloat16),
            pltpu.VMEM((768, 256), jnp.bfloat16),
            pltpu.VMEM((1536, 512), jnp.bfloat16),
            pltpu.SemaphoreType.DMA((8,)),
        ],
        compiler_params=params(16),
        cost_estimate=pl.CostEstimate(
            flops=1610612736, bytes_accessed=4000000, transcendentals=0
        ),
        name="ladder",
    )(place, *turns, factor, other)


def turned(value):
    return [value] + [
        lax.ppermute(value, "vert", [(v, (v + 2 * turn) % 8) for v in range(8)])
        for turn in range(1, 4)
    ]


def swapped(value):
    return lax.ppermute(value, "vert", [(v, v ^ 1) for v in range(8)])


def passed(value):
    return lax.ppermute(value, "ka", [(k, (k + 1) % 64) for k in range(64)])


def ahead(value):
    pairs = [
        (k * 8 + v, (k + 1) * 8 + v if k < 63 else v ^ 1) for k in range(64) for v in range(8)
    ]
    return lax.ppermute(value, ("ka", "vert"), pairs)


def per_device(amplitudes, factors, kminus, kj_rows, kshift):
    vert = lax.axis_index("vert")
    high = lax.rem(vert, 2)
    level = lax.div(vert, 2)
    rank = jnp.array(RANK, jnp.int32)
    lookup = (rank, kminus, kj_rows, kshift)
    place = jnp.stack([lax.rem(level + 4 - turn, 4) * 32 for turn in range(4)]).astype(jnp.int32)

    row = lax.div(rank[lax.axis_index("ka")], 32).reshape(1)

    shard = amplitudes[:, 0]
    spread = exchange(
        jnp.concatenate([factors[:, 0].reshape(64, 6, 4, 128), shard.reshape(64, 1, 4, 128)], 1)
    )
    behind = passed(shard)
    spread, behind = lax.optimization_barrier((spread, behind))

    mirror = exchange_both(mirror_pieces(lookup, row, spread))
    here = jnp.stack([shard, behind]).reshape(2, 16, 16, 128)
    chosen = factor_pieces(lookup, spread)
    here, chosen = lax.optimization_barrier((here, chosen))
    there = swapped(here)
    mirror, chosen = lax.optimization_barrier((mirror, chosen))

    other = exchange(chosen.reshape(64, 48, 128))
    mirror = mirror.reshape(2, 16, 16, 128)
    turns = turned(
        joined(high.astype(jnp.int32).reshape(1), here, there, mirror, ahead(mirror))
    )
    partial = ladder(place, turns, factors[:, 0], other)

    groups = [[0, 2, 4, 6], [1, 3, 5, 7]]
    pieces = lax.all_to_all(
        partial, "vert", split_axis=0, concat_axis=0, tiled=True, axis_index_groups=groups
    )
    total = jnp.sum(pieces.astype(jnp.float32), 0).reshape(2, 4, 2, 2, 16, 128)
    keep = jnp.where(high == 0, total[:, :, :, 0], total[:, :, :, 1])
    give = jnp.where(high == 0, total[:, :, :, 1], total[:, :, :, 0]).astype(jnp.bfloat16)
    taken = swapped(give)
    total = (keep + taken.astype(jnp.float32)).astype(jnp.bfloat16)
    return total[:, None]


def solution(mesh):
    in_specs = (
        P(None, "ka", None, None, "vert", None),
        P(None, "ka", None, "vert", None, None),
        P(),
        P(),
        P(),
    )
    out_specs = P(None, "ka", None, None, "vert", None)
    return jax.shard_map(
        per_device, mesh=mesh, in_specs=in_specs, out_specs=out_specs, check_vma=False
    )
```

```python
import jax
import jax.numpy as jnp
from jax import lax
from jax.experimental import pallas as pl
from jax.experimental.pallas import tpu as pltpu
from jax.sharding import PartitionSpec as P

ORDER = [
    29, 59, 17, 8, 28, 7, 44, 46, 23, 57, 24, 21, 51, 43, 47, 19,
    31, 55, 4, 1, 15, 14, 45, 37, 26, 9, 42, 62, 61, 20, 16, 38,
    54, 41, 32, 30, 33, 39, 36, 35, 53, 18, 50, 56, 40, 0, 10, 63,
    34, 25, 13, 5, 52, 60, 22, 48, 12, 58, 3, 2, 49, 6, 27, 11,
]
RANK = [ORDER.index(k) for k in range(64)]

SMEM = pl.BlockSpec(memory_space=pltpu.SMEM)
VMEM = pl.BlockSpec(memory_space=pltpu.VMEM)
ANY = pl.BlockSpec(memory_space=pl.ANY)


def params(mebibytes):
    return pltpu.CompilerParams(vmem_limit_bytes=mebibytes * 1024 * 1024)


def wide(value):
    return value.astype(jnp.float32)


def exchange(value):
    return lax.all_to_all(
        value, "ka", split_axis=0, concat_axis=0, tiled=True, axis_index_groups=[ORDER]
    )


def exchange_both(value):
    groups = [[k * 8 + 2 * y + h for h in range(2) for k in ORDER] for y in range(4)]
    return lax.all_to_all(
        value, ("ka", "vert"), split_axis=0, concat_axis=0, tiled=True, axis_index_groups=groups
    )


def pack_kernel(factor_ref, shard_ref, out_ref, held, done):
    first = pltpu.make_async_copy(factor_ref, held.at[:, 0:6], done.at[0])
    second = pltpu.make_async_copy(shard_ref, held.at[:, 6:7], done.at[1])
    first.start()
    second.start()
    first.wait()
    second.wait()
    last = pltpu.make_async_copy(held, out_ref, done.at[2])
    last.start()
    last.wait()


def packed(factor, shard):
    return pl.pallas_call(
        pack_kernel,
        out_shape=jax.ShapeDtypeStruct((64, 7, 4, 128), jnp.bfloat16),
        in_specs=[ANY, ANY],
        out_specs=ANY,
        scratch_shapes=[
            pltpu.VMEM((64, 7, 4, 128), jnp.bfloat16),
            pltpu.SemaphoreType.DMA((3,)),
        ],
        compiler_params=params(56),
        cost_estimate=pl.CostEstimate(flops=0, bytes_accessed=900000, transcendentals=0),
        name="packed",
    )(factor, shard)


def join_kernel(high_ref, here_ref, there_ref, now_ref, before_ref, out_ref, done):
    high = high_ref[0]
    copies = [
        pltpu.make_async_copy(here_ref, out_ref.at[pl.ds(0, 2), high], done.at[0]),
        pltpu.make_async_copy(there_ref, out_ref.at[pl.ds(0, 2), 1 - high], done.at[1]),
        pltpu.make_async_copy(now_ref, out_ref.at[2], done.at[2]),
        pltpu.make_async_copy(before_ref, out_ref.at[3], done.at[3]),
    ]
    for copy in copies:
        copy.start()
    for copy in copies:
        copy.wait()


def joined(high, *parts):
    return pl.pallas_call(
        join_kernel,
        out_shape=jax.ShapeDtypeStruct((4, 2, 16, 16, 128), jnp.bfloat16),
        in_specs=[SMEM] + [ANY] * 4,
        out_specs=VMEM,
        scratch_shapes=[pltpu.SemaphoreType.DMA((4,))],
        compiler_params=params(8),
        cost_estimate=pl.CostEstimate(
            flops=115000000000, bytes_accessed=1000000, transcendentals=0
        ),
        name="joined",
    )(high, *parts)


def mirror_kernel(rank_ref, kminus_ref, rows_ref, shift_ref, row_ref, spread_ref, out_ref):
    target = kminus_ref[rows_ref[row_ref[0]], shift_ref[0]]
    for at, k in enumerate(ORDER):
        piece = spread_ref[rank_ref[kminus_ref[target, k]], 6]
        out_ref[at] = piece
        out_ref[64 + at] = piece


def mirror_pieces(lookup, row, spread):
    return pl.pallas_call(
        mirror_kernel,
        out_shape=jax.ShapeDtypeStruct((128, 4, 128), jnp.bfloat16),
        in_specs=[SMEM] * 5 + [VMEM],
        out_specs=VMEM,
        compiler_params=params(12),
        cost_estimate=pl.CostEstimate(flops=0, bytes_accessed=700000, transcendentals=0),
        name="mirror_pieces",
    )(*lookup, row, spread)


def factor_kernel(rank_ref, kminus_ref, rows_ref, shift_ref, spread_ref, out_ref):
    for row in range(2):
        target = kminus_ref[rows_ref[row], shift_ref[0]]
        for at, k in enumerate(ORDER):
            out_ref[at, row * 6 : row * 6 + 6] = spread_ref[
                rank_ref[kminus_ref[target, k]], 0:6
            ]


def factor_pieces(lookup, spread):
    return pl.pallas_call(
        factor_kernel,
        out_shape=jax.ShapeDtypeStruct((64, 12, 4, 128), jnp.bfloat16),
        in_specs=[SMEM] * 4 + [VMEM],
        out_specs=VMEM,
        compiler_params=params(12),
        cost_estimate=pl.CostEstimate(flops=0, bytes_accessed=1300000, transcendentals=0),
        name="factor_pieces",
    )(*lookup, spread)


def complex_matrix(real, imag):
    return jnp.concatenate(
        [jnp.concatenate([real, -imag], 1), jnp.concatenate([imag, real], 1)], 0
    )


def ladder_kernel(place_ref, *refs):
    turns = refs[0:4]
    factor_ref, other_ref, out_ref, blocks, left, right, inner, result, arrived, leaving = refs[4:14]
    copies = []
    for turn in range(4):
        for high in range(2):
            start = pl.multiple_of(place_ref[turn] + high * 16, 16)
            copies.append(
                pltpu.make_async_copy(
                    turns[turn].at[:, high],
                    blocks.at[:, :, pl.ds(start, 16), :],
                    arrived.at[turn * 2 + high],
                )
            )
    for copy in copies:
        copy.start()
    for step in range(2):
        for lane in range(3):
            at = (step * 3 + lane) * 256
            left[:, at : at + 256] = complex_matrix(
                factor_ref[step, 0, lane], factor_ref[step, 1, lane]
            )
    for copy in copies:
        copy.wait()
    leaves = []
    for row in range(2):
        other = jnp.concatenate(
            [wide(other_ref[m])[row * 24 : (row + 1) * 24] for m in range(64)], 0
        ).astype(jnp.bfloat16)
        for step in range(2):
            for lane in range(3):
                real = (step * 6 + lane) * 128
                imag = real + 384
                right[lane * 256 : (lane + 1) * 256, :] = complex_matrix(
                    other[real : real + 128], other[imag : imag + 128]
                )
            tilde = []
            for occ in range(4):
                parts = []
                for part in range(2):
                    block = (row * 4 + occ) * 2 + part
                    flipped = jnp.transpose(wide(blocks[2 + step, block]))
                    value = 2.0 * wide(blocks[step, block]) - flipped
                    parts.append(value.astype(jnp.bfloat16))
                tilde.append(jnp.concatenate(parts, 1))
            product = lax.dot_general(
                jnp.concatenate(tilde, 0),
                right[...],
                (((1,), (1,)), ((), ())),
                preferred_element_type=jnp.float32,
            ).astype(jnp.bfloat16)
            for lane in range(3):
                for part in range(2):
                    at = (step * 3 + lane) * 256 + part * 128
                    column = lane * 256 + part * 128
                    for occ in range(4):
                        inner[at : at + 128, occ * 128 : (occ + 1) * 128] = product[
                            occ * 128 : (occ + 1) * 128, column : column + 128
                        ]
        total = jnp.dot(left[...], inner[...], preferred_element_type=jnp.float32)
        total = total.astype(jnp.bfloat16)
        for occ in range(4):
            for part in range(2):
                for place in range(4):
                    at = part * 128 + place * 32
                    result[row, place, occ, part] = total[
                        at : at + 32, occ * 128 : (occ + 1) * 128
                    ]
        copies = [
            pltpu.make_async_copy(
                result.at[row, place], out_ref.at[place, row], leaving.at[row * 4 + place]
            )
            for place in range(4)
        ]
        for copy in copies:
            copy.start()
        leaves = leaves + copies
    for copy in leaves:
        copy.wait()


def ladder(place, turns, factor, other):
    return pl.pallas_call(
        ladder_kernel,
        out_shape=jax.ShapeDtypeStruct((4, 2, 4, 2, 32, 128), jnp.bfloat16),
        in_specs=[SMEM] + [ANY] * 4 + [VMEM, VMEM],
        out_specs=ANY,
        scratch_shapes=[
            pltpu.VMEM((4, 16, 128, 128), jnp.bfloat16),
            pltpu.VMEM((256, 1536), jnp.bfloat16),
            pltpu.VMEM((768, 256), jnp.bfloat16),
            pltpu.VMEM((1536, 512), jnp.bfloat16),
            pltpu.VMEM((2, 4, 4, 2, 32, 128), jnp.bfloat16),
            pltpu.SemaphoreType.DMA((8,)),
            pltpu.SemaphoreType.DMA((8,)),
        ],
        compiler_params=params(16),
        cost_estimate=pl.CostEstimate(
            flops=1610612736, bytes_accessed=4000000, transcendentals=0
        ),
        name="ladder",
    )(place, *turns, factor, other)


def turned(value):
    return [value] + [
        lax.ppermute(value, "vert", [(v, (v + 2 * turn) % 8) for v in range(8)])
        for turn in range(1, 4)
    ]


def swapped(value):
    return lax.ppermute(value, "vert", [(v, v ^ 1) for v in range(8)])


def passed(value):
    return lax.ppermute(value, "ka", [(k, (k + 1) % 64) for k in range(64)])


def ahead(value):
    pairs = [
        (k * 8 + v, (k + 1) * 8 + v if k < 63 else v ^ 1) for k in range(64) for v in range(8)
    ]
    return lax.ppermute(value, ("ka", "vert"), pairs)


def per_device(amplitudes, factors, kminus, kj_rows, kshift):
    vert = lax.axis_index("vert")
    high = lax.rem(vert, 2)
    level = lax.div(vert, 2)
    rank = jnp.array(RANK, jnp.int32)
    lookup = (rank, kminus, kj_rows, kshift)
    place = jnp.stack([lax.rem(level + 4 - turn, 4) * 32 for turn in range(4)]).astype(jnp.int32)

    row = lax.div(rank[lax.axis_index("ka")], 32).reshape(1)

    shard = amplitudes[:, 0]
    spread = exchange(
        packed(factors[:, 0].reshape(64, 6, 4, 128), shard.reshape(64, 1, 4, 128))
    )
    behind = passed(shard)
    spread, behind = lax.optimization_barrier((spread, behind))

    mirror = exchange_both(mirror_pieces(lookup, row, spread))
    here = jnp.stack([shard, behind]).reshape(2, 16, 16, 128)
    chosen = factor_pieces(lookup, spread)
    here, chosen = lax.optimization_barrier((here, chosen))
    there = swapped(here)
    mirror, chosen = lax.optimization_barrier((mirror, chosen))

    other = exchange(chosen.reshape(64, 48, 128))
    mirror = mirror.reshape(2, 16, 16, 128)
    turns = turned(
        joined(high.astype(jnp.int32).reshape(1), here, there, mirror, ahead(mirror))
    )
    partial = ladder(place, turns, factors[:, 0], other)

    groups = [[0, 2, 4, 6], [1, 3, 5, 7]]
    pieces = lax.all_to_all(
        partial, "vert", split_axis=0, concat_axis=0, tiled=True, axis_index_groups=groups
    )
    total = jnp.sum(pieces.astype(jnp.float32), 0).reshape(2, 4, 2, 2, 16, 128)
    keep = jnp.where(high == 0, total[:, :, :, 0], total[:, :, :, 1])
    give = jnp.where(high == 0, total[:, :, :, 1], total[:, :, :, 0]).astype(jnp.bfloat16)
    taken = swapped(give)
    total = (keep + taken.astype(jnp.float32)).astype(jnp.bfloat16)
    return total[:, None]


def solution(mesh):
    in_specs = (
        P(None, "ka", None, None, "vert", None),
        P(None, "ka", None, "vert", None, None),
        P(),
        P(),
        P(),
    )
    out_specs = P(None, "ka", None, None, "vert", None)
    return jax.shard_map(
        per_device, mesh=mesh, in_specs=in_specs, out_specs=out_specs, check_vma=False
    )
```
